32 devices in a mesh: img: 4 (over y, core), term: 8 (over z, x).
Axes of the slice: x: 2, y: 2, z: 4, core: 2. Of those that a mesh axis runs over, the one named last changes fastest.
Arguments:
- patches: bfloat16 [16, 256, 1024], P('img', 'term'), may hold values from -6 to 6
- patch_mask: int32 [16, 256], P('img', 'term'), may hold values 0 or 1
- proj_weight: bfloat16 [1024, 30720], P('img', 'term'), may hold values from -0.1875 to 0.1875
- proj_bias: float32 [30720], P('term'), may hold values from -4 to 4
- slab: bfloat16 [2032, 30720], P('img', 'term'), may hold values from 0 to 2
- query_ids: int32 [1024, 32], replicated, may hold values from -1 to 30719, as said below
- term_weights: bfloat16 [1024, 32], replicated, may hold values from 0.25 to 4
Outputs:
- scores: float32 [1024, 2048], P('term', 'img')
The draws below stay inside these ranges and needn't reach their ends.
Inputs may be any that keep to these rules, and one draw needn't show every extreme that they name: `query_ids`: within a query the non-negative ids are distinct and come before the padding slots; every query has at least 8 real terms and some query fills all 32 slots.
All inputs are finite; a program needn't handle non-finite values. No bound on the sum of `patch_mask` on one device may be relied on, other than what follows from the above.
Results may differ from the reference program's by a relative error of at most 0.0003.
Values may be sent and summed in bfloat16 or wider, within the bound.
No kernel may reach another device: no remote copies, remote signals or barrier semaphores. Data moves between devices by JAX's collectives and lax.ppermute only.
A program may use at most 64 MiB of HBM per device.

```python
import math
import jax
import jax.numpy as jnp
from jax import lax

D = 1024
V = 30720
P_SIZE = 256
L = 32
Q = 1024
NEW_DEV = 4
SLAB_DEV = 508
NEW = 16
SLAB = 2032
IMGS = 2048
N_IMG = 4


def draw_query_ids(key, part):
    key_len = jax.random.fold_in(key, 11)
    key_pick = jax.random.fold_in(key, 12)
    key_rank = jax.random.fold_in(key, 13)
    lengths = jax.random.randint(key_len, (Q,), L // 4, L + 1)
    chosen = jax.random.randint(key_pick, (), 0, Q)
    lengths = jnp.where(jnp.arange(Q) == chosen, L, lengths)
    ranking = jax.random.randint(key_rank, (Q, V), 0, 2 ** 30 // V) * V + jnp.arange(V, dtype=jnp.int32)[None, :]
    _, chosen_ids = lax.top_k(ranking, L)
    slots = jnp.arange(L)[None, :]
    return jnp.where(slots < lengths[:, None], chosen_ids, -1).astype(jnp.int32)


def touch_ends(values, stream_key, least, largest):
    longest = values.shape.index(max(values.shape))
    spots = []
    for shift in (0, 1):
        where = [jax.random.randint(jax.random.fold_in(stream_key, axis), (), 0, length) for axis, length in enumerate(values.shape)]
        where[longest] = (where[longest] + shift) % values.shape[longest]
        spots.append(tuple(where))
    return values.at[spots[0]].set(least).at[spots[1]].set(largest)


def shard_levels(rng, shape, split, least, largest):
    gain, own = 1.0, jax.random.fold_in(rng, 6)
    for dim, parts in split:
        heights = jnp.exp(jax.random.uniform(jax.random.fold_in(own, dim), (parts,), jnp.float32, least / len(split), largest / len(split)))
        gain = gain * jnp.repeat(heights, shape[dim] // parts).reshape([-1 if axis == dim else 1 for axis in range(len(shape))])
    return gain


def gaussian(key, shape, scale, reach, pieces=(), kind=jnp.bfloat16):
    values = scale * jax.random.normal(key, shape, jnp.float32)
    if pieces:
        values = values * shard_levels(key, shape, pieces, -0.22, 0.18)
    return jnp.clip(values, -reach, reach).astype(kind)


def setup_inputs(seed: int = 0) -> dict:
    key_of = jax.random.split(jax.random.key(seed), 8)
    return {
        "patches": gaussian(key_of[0], (NEW, P_SIZE, D), 1.0, 6.0, ((0, 4), (1, 8))),
        "patch_mask": touch_ends((jax.random.randint(key_of[1], (NEW, P_SIZE), 0, 4) < 3).astype(jnp.int32), jax.random.fold_in(key_of[1], 1), 0, 1),
        "proj_weight": gaussian(key_of[2], (D, V), D ** -0.5, 0.1875, ((0, 4), (1, 8))),
        "proj_bias": gaussian(key_of[3], (V,), 1.0, 4.0, ((0, 8),), jnp.float32),
        "slab": jnp.clip(2.0 * jax.random.uniform(key_of[4], (SLAB, V), jnp.float32) ** shard_levels(key_of[4], (SLAB, V), ((0, 4), (1, 8)), -0.2, 0.2), 0.0, 2.0).astype(jnp.bfloat16),
        "query_ids": draw_query_ids(jax.random.fold_in(key_of[7], 71), 0),
        "term_weights": jnp.clip(jnp.exp(jax.random.uniform(key_of[6], (Q, L), jnp.float32, math.log(0.25), math.log(4.0))), 0.25, 4.0).astype(jnp.bfloat16),
    }


def one_image(pair, proj_weight, proj_bias):
    features, keep_mask = pair
    logits = jnp.dot(features, proj_weight, preferred_element_type=jnp.float32) + proj_bias
    activity = jnp.log1p(jnp.maximum(logits, 0.0))
    activity = jnp.where(keep_mask[:, None] > 0, activity, 0.0)
    return jnp.max(activity, axis=0)


def reference(patches, patch_mask, proj_weight, proj_bias, slab, query_ids, term_weights):
    new_impacts = lax.map(lambda pair: one_image(pair, proj_weight, proj_bias), (patches, patch_mask))
    new_impacts = new_impacts.astype(jnp.bfloat16)
    impacts = jnp.concatenate([slab.reshape(N_IMG, SLAB_DEV, V), new_impacts.reshape(N_IMG, NEW_DEV, V)], axis=1)
    impacts = impacts.reshape(IMGS, V)
    query_weight = jnp.where(query_ids >= 0, term_weights, jnp.zeros((), jnp.bfloat16)).astype(jnp.bfloat16)
    safe_ids = jnp.maximum(query_ids, 0).astype(jnp.int32)
    blocks = Q // 64 if Q % 64 == 0 else Q
    rows_block = Q // blocks

    def score_block(pair):
        ids_block, weight_block = pair
        picked = jnp.take(impacts, ids_block, axis=1).astype(jnp.float32)
        return jnp.sum(picked * weight_block.astype(jnp.float32)[None], axis=2).T

    result = lax.map(score_block, (safe_ids.reshape(blocks, rows_block, L), query_weight.reshape(blocks, rows_block, L)))
    return result.reshape(Q, IMGS)
```

```python
import functools

import jax
import jax.numpy as jnp
from jax import lax
from jax.experimental import pallas as pl
from jax.experimental.pallas import tpu as pltpu
from jax.sharding import Mesh, PartitionSpec as P

BF16 = jnp.bfloat16
F32 = jnp.float32
LANES = 128
WIDE = 256
GROUP = 8
ROWS_BY_ROWS = (((1,), (1,)), ((), ()))
VMEM_BYTES = 48 << 20


def whole(array):
    return pl.BlockSpec(array.shape, lambda i, *_: (0,) * array.ndim)


def expand_terms(slots, blocks, width, base, ids, weights, out, row):
    query = lax.broadcasted_iota(jnp.int32, (1, GROUP * slots), 1) // slots
    parts = []
    for g in range(2):
        local = ids[pl.ds(2 * row + g, 1), :] - base
        inside = (local >= 0) & (local < width)
        key = jnp.where(inside, (local // WIDE) * GROUP + query, -1)
        rows = lax.broadcasted_iota(jnp.int32, (blocks * GROUP, GROUP * slots), 0)
        coarse = jnp.where(rows == key, weights[pl.ds(2 * row + g, 1), :], 0.0).astype(BF16)
        place = lax.broadcasted_iota(jnp.int32, (WIDE, GROUP * slots), 0)
        fine = jnp.where(place == (local & (WIDE - 1)), 1.0, 0.0).astype(BF16)
        parts.append(
            lax.dot_general(coarse, fine, ROWS_BY_ROWS, preferred_element_type=F32)
        )
    start = pl.multiple_of(row * 2 * GROUP, 2 * GROUP)
    for b in range(blocks):
        pair = [part[b * GROUP : (b + 1) * GROUP] for part in parts]
        out[pl.ds(start, 2 * GROUP), b * WIDE : (b + 1) * WIDE] = jnp.concatenate(
            pair, axis=0
        ).astype(BF16)


def score_kernel(slots, place, ids, weights, slab, dense, *rest):
    *outs, scores = rest
    images, width = slab.shape
    base, z = place[0], place[1]
    blocks = dense.shape[1] // WIDE
    steps = ids.shape[0] // 2

    def step(row, carry):
        expand_terms(slots, blocks, width, base, ids, weights, dense, row)
        return carry

    lax.fori_loop(0, steps, step, 0, unroll=8 if steps % 8 == 0 else 1)
    found = lax.dot_general(
        dense[:, :width], slab[...], ROWS_BY_ROWS, preferred_element_type=F32
    )
    scores[...] = found.reshape(scores.shape)
    for k, out in enumerate(outs):
        out[:, :images] = scores[jnp.bitwise_xor(z, k)]
        out[:, images:] = jnp.zeros((out.shape[0], out.shape[1] - images), F32)


def score_slab(place, ids, weights, slab, slots, depth, images):
    groups = ids.shape[0]
    queries = groups * GROUP
    held, width = slab.shape
    padded = -(-width // WIDE) * WIDE
    rows = queries // depth
    dense = jax.ShapeDtypeStruct((queries, padded), BF16)
    part = jax.ShapeDtypeStruct((rows, images), F32)
    return pl.pallas_call(
        functools.partial(score_kernel, slots),
        grid_spec=pltpu.PrefetchScalarGridSpec(
            num_scalar_prefetch=1,
            grid=(1,),
            in_specs=[whole(ids), whole(weights), whole(slab)],
            out_specs=[whole(dense)] + [whole(part)] * depth,
            scratch_shapes=[pltpu.VMEM((depth, rows, held), F32)],
        ),
        out_shape=[dense] + [part] * depth,
        compiler_params=pltpu.CompilerParams(vmem_limit_bytes=VMEM_BYTES),
        cost_estimate=pl.CostEstimate(
            flops=2 * queries * width * images * 3, bytes_accessed=12 << 20, transcendentals=0
        ),
        name="score_slab",
    )(place, ids, weights, slab)


def project_kernel(pieces, parts, aligned, images, patches, place, *refs):
    own, peer = refs[0], refs[1]
    weights = refs[2 : 2 + pieces]
    bias = refs[2 + pieces]
    dense = refs[3 + pieces : 3 + pieces + parts]
    running, out, gathered, best, wide, arrived = refs[3 + pieces + parts :]
    i = pl.program_id(0)
    steps = pl.num_programs(0) // 2
    depth, columns = weights[0].shape
    index, core, x, offset = place[0], place[1], place[2], place[3]

    def fetch(k):
        source = dense[k]
        if aligned:
            source = source.at[:, pl.ds(pl.multiple_of(offset, LANES), columns)]
        return pltpu.make_async_copy(source, wide.at[k], arrived.at[k])

    @pl.when(i == 0)
    def _():
        for k in range(parts):
            fetch(k).start()
        for k, piece in enumerate(weights):
            at = jnp.bitwise_xor(index, k) * depth
            gathered[pl.ds(pl.multiple_of(at, depth), depth), :] = piece[...]
        best[...] = jnp.full(best.shape, -jnp.inf, F32)

    def pool(block, side):
        logits = jnp.dot(block[...], gathered[...], preferred_element_type=F32)
        real = block[:, 0:1].astype(F32) < jnp.inf
        logits = jnp.where(real, logits, -jnp.inf)
        logits = logits.reshape(-1, images, patches, columns)
        best[side] = jnp.maximum(best[side], jnp.max(jnp.max(logits, axis=2), axis=0))

    @pl.when(i < steps)
    def _():
        pool(own, 0)

    @pl.when(i >= steps)
    def _():
        pool(peer, 1)

    @pl.when(i == 2 * steps - 1)
    def _():
        active = jnp.log1p(jnp.maximum(best[...] + bias[...], 0.0))
        pooled = jnp.concatenate([active[0], active[1]], axis=0).astype(BF16)
        out[...] = running[...]
        depth_z, queries = out.shape[1], out.shape[4]
        for k in range(parts):
            fetch(k).wait()
            found = lax.dot_general(pooled, wide[k], ROWS_BY_ROWS, preferred_element_type=F32)
            at = jnp.bitwise_xor(x, k)
            for z in range(depth_z):
                mine = found[:, z * queries : (z + 1) * queries]
                for side in range(2):
                    spot = (jnp.bitwise_xor(core, side), z, at, slice(0, images))
                    out[spot] = out[spot] + mine[side * images : (side + 1) * images]


def project(place, own, peer, weights, bias, dense, running, aligned, images, patches):
    rows, features = own.shape
    block = 512 if rows % 512 == 0 else rows
    steps = rows // block
    depth, columns = weights[0].shape
    queries = dense[0].shape[0]
    return pl.pallas_call(
        functools.partial(
            project_kernel, len(weights), len(dense), aligned, images, patches
        ),
        grid_spec=pltpu.PrefetchScalarGridSpec(
            num_scalar_prefetch=1,
            grid=(2 * steps,),
            in_specs=[
                pl.BlockSpec((block, features), lambda i, s: (jnp.minimum(i, steps - 1), 0)),
                pl.BlockSpec((block, features), lambda i, s: (jnp.maximum(i - steps, 0), 0)),
            ]
            + [whole(w) for w in weights]
            + [whole(bias)]
            + [pl.BlockSpec(memory_space=pl.ANY)] * len(dense)
            + [whole(running)],
            out_specs=whole(running),
            scratch_shapes=[
                pltpu.VMEM((features, columns), BF16),
                pltpu.VMEM((2, images, columns), F32),
                pltpu.VMEM((len(dense), queries, columns), BF16),
                pltpu.SemaphoreType.DMA((len(dense),)),
            ],
        ),
        out_shape=jax.ShapeDtypeStruct(running.shape, F32),
        compiler_params=pltpu.CompilerParams(vmem_limit_bytes=VMEM_BYTES),
        cost_estimate=pl.CostEstimate(
            flops=4 * rows * features * columns, bytes_accessed=8 << 20, transcendentals=0
        ),
        name="project",
    )(place, own, peer, *weights, bias, *dense, running)


def column_blocks(width):
    if width % LANES or width < 4 * LANES:
        return [(0, width)]
    tiles = width // LANES
    sizes, left = [], tiles
    for share in (3, 2, 2):
        take = max(1, left // share) if left > 1 else left
        if take:
            sizes.append(take)
            left -= take
    if left:
        sizes.append(left)
    sizes.sort(reverse=True)
    blocks, start = [], 0
    for size in sizes:
        blocks.append((start * LANES, size * LANES))
        start += size
    return blocks


def shards(rows, terms, patches, patch_mask, proj_weight, proj_bias, slab, query_ids, term_weights):
    along_x = 1
    while along_x * along_x * 4 <= terms:
        along_x *= 2
    along_z = terms // along_x
    row, core, term = lax.axis_index("row"), lax.axis_index("core"), lax.axis_index("term")
    x, z = term % along_x, term // along_x
    images, patch_rows, features = patches.shape
    depth, width = proj_weight.shape
    held = slab.shape[0]
    slots = query_ids.shape[1]
    block_queries = query_ids.shape[0] // terms

    def to_term(value, k):
        return lax.ppermute(value, "term", [(i, i ^ k) for i in range(terms)])

    def to_row(value, k, flip):
        return lax.ppermute(
            value, ("row", "core"), [(i, i ^ (2 * k + flip)) for i in range(2 * rows)]
        )

    half = width // 2
    blocks = column_blocks(half)
    pieces = []
    for start, size in blocks:
        mine = lax.dynamic_slice(proj_weight, (0, core * half + start), (depth, size))
        other = lax.dynamic_slice(proj_weight, (0, (1 - core) * half + start), (depth, size))
        got = [mine]
        for k in range(1, 2 * rows):
            got.append(to_row(other if k % 2 else mine, k // 2, k % 2))
        pieces.append(got)

    marked = jnp.where(patch_mask[:, :, None] > 0, patches, jnp.array(jnp.inf, BF16))
    columns_z = [marked] + [to_term(marked, k * along_x) for k in range(1, along_z)]
    everything = list(columns_z)
    for k in range(1, along_x):
        everything += [to_term(block, k) for block in columns_z]
    own = jnp.stack(everything).reshape(terms * images * patch_rows, features)
    peer = to_row(own, 0, 1)

    ids = query_ids.reshape(along_z, along_x, block_queries, slots)
    weights = jnp.where(query_ids >= 0, term_weights, jnp.zeros((), BF16)).astype(F32)
    weights = weights.reshape(ids.shape)
    place = jnp.stack([term * width, z]).astype(jnp.int32)
    dense, summed = [], None
    for k in [*range(1, along_x), 0]:
        picked = [
            lax.dynamic_index_in_dim(a, x ^ k, 1, keepdims=False).reshape(-1, GROUP * slots)
            for a in (ids, weights)
        ]
        full, *parts = score_slab(
            place, *picked, slab, slots, along_z, held + images
        )
        dense.append((k, full))
        if k:
            parts = [to_term(part, k) for part in parts]
        summed = parts if summed is None else [a + b for a, b in zip(summed, parts)]
    dense = [full for _, full in sorted(dense, key=lambda pair: pair[0])]
    stored = summed[0]
    for k in range(1, along_z):
        stored = stored + to_term(summed[k], k * along_x)

    running = jnp.zeros((2, along_z, along_x, 8, block_queries), F32)
    bias = proj_bias.reshape(1, width)
    aligned = half % LANES == 0
    for (start, size), got in zip(blocks, pieces):
        offset = core * half + start
        place = jnp.stack([2 * row + core, core, x, offset]).astype(jnp.int32)
        spans = dense
        if not aligned:
            spans = [lax.dynamic_slice(d, (0, offset), (d.shape[0], size)) for d in dense]
        running = project(
            place, own, peer, got, lax.dynamic_slice(bias, (0, offset), (1, size)),
            spans, running, aligned, images, patch_rows,
        )
    sent = running.reshape(2 * terms, 8, block_queries)
    fresh = lax.all_to_all(sent, ("core", "term"), split_axis=0, concat_axis=0, tiled=True)
    fresh = jnp.sum(fresh, axis=0)[:images].T
    return jnp.concatenate([stored[:, :held], fresh], axis=1)


def solution(mesh):
    groups, terms = mesh.shape["img"], mesh.shape["term"]
    rows = groups // 2
    cores = Mesh(mesh.devices.reshape(rows, 2, terms), ("row", "core", "term"))
    img = ("row", "core")
    placed = (
        P(img, "term", None),
        P(img, "term"),
        P(img, "term"),
        P("term"),
        P(img, "term"),
        P(),
        P(),
    )
    return jax.shard_map(
        functools.partial(shards, rows, terms),
        mesh=cores,
        in_specs=placed,
        out_specs=P("term", img),
        check_vma=False,
    )
```

```python
import functools

import jax
import jax.numpy as jnp
from jax import lax
from jax.experimental import pallas as pl
from jax.experimental.pallas import tpu as pltpu
from jax.sharding import Mesh, PartitionSpec as P

BF16 = jnp.bfloat16
F32 = jnp.float32
LANES = 128
WIDE = 256
GROUP = 8
ROWS_BY_ROWS = (((1,), (1,)), ((), ()))
VMEM_BYTES = 61 << 20
LEVELS, OFFSET, TINY = 65535.0, 32768, 1e-30
PARTS = 2
K1COST = 9 << 30
TILE = 768
BRIEF = pl.CostEstimate(flops=1024, bytes_accessed=1024, transcendentals=0)


def whole(array):
    return pl.BlockSpec(array.shape, lambda i, *_: (0,) * array.ndim)


def expand_terms(slots, blocks, width, base, ids, weights, out, row):
    query = lax.broadcasted_iota(jnp.int32, (1, GROUP * slots), 1) // slots
    parts = []
    for g in range(2):
        local = ids[pl.ds(2 * row + g, 1), :] - base
        inside = (local >= 0) & (local < width)
        key = jnp.where(inside, (local // WIDE) * GROUP + query, -1)
        rows = lax.broadcasted_iota(jnp.int32, (blocks * GROUP, GROUP * slots), 0)
        coarse = jnp.where(rows == key, weights[pl.ds(2 * row + g, 1), :], 0.0).astype(BF16)
        place = lax.broadcasted_iota(jnp.int32, (WIDE, GROUP * slots), 0)
        fine = jnp.where(place == (local & (WIDE - 1)), 1.0, 0.0).astype(BF16)
        parts.append(
            lax.dot_general(coarse, fine, ROWS_BY_ROWS, preferred_element_type=F32)
        )
    start = pl.multiple_of(row * 2 * GROUP, 2 * GROUP)
    for b in range(blocks):
        pair = [part[b * GROUP : (b + 1) * GROUP] for part in parts]
        out[pl.ds(start, 2 * GROUP), b * WIDE : (b + 1) * WIDE] = jnp.concatenate(
            pair, axis=0
        ).astype(BF16)


def score_kernel(place, query_ids, term_weights, slab, *refs):
    dense, coded, scales, whole_row, stored, weighed, ids, weights, came = refs[-9:]
    slots = query_ids.shape[1]
    images, width = slab.shape
    terms, queries, _ = coded.shape
    blocks = dense.shape[1] // WIDE
    steps = ids.shape[0] // 2
    fetch = pltpu.make_async_copy(slab, stored, came)
    fetch.start()
    weighed[...] = jnp.where(query_ids[...] >= 0, term_weights[...].astype(F32), 0.0)
    for q in range(GROUP):
        rows = pl.ds(q, ids.shape[0], stride=GROUP)
        ids[:, q * slots : (q + 1) * slots] = query_ids[rows, :]
        weights[:, q * slots : (q + 1) * slots] = weighed[rows, :]

    def step(row, carry):
        expand_terms(slots, blocks, width, place[0], ids, weights, dense, row)
        return carry

    lax.fori_loop(0, steps, step, 0, unroll=8 if steps % 8 == 0 else 1)
    fetch.wait()
    found = lax.dot_general(
        dense[:, :width], stored[...], ROWS_BY_ROWS, preferred_element_type=F32
    )
    lane = lax.broadcasted_iota(jnp.int32, (queries, LANES), 1)
    tops = jnp.zeros((queries, LANES), F32)
    whole_row[...] = jnp.zeros(whole_row.shape, F32)
    for t in range(terms):
        part = found[t * queries : (t + 1) * queries]
        top = jnp.maximum(jnp.max(part, axis=1, keepdims=True), TINY)
        whole_row[:, :images] = part * (LEVELS / top) + 0.5
        coded[t] = (whole_row[...].astype(jnp.int32) - OFFSET).astype(jnp.int16)
        tops = jnp.where(lane == t, top * (1.0 / LEVELS), tops)
    scales[...] = jnp.swapaxes(tops, 0, 1)[: scales.shape[0]]


def score_slab(place, ids, weights, slab, terms, images, part, parts, coded):
    queries, slots = ids.shape[0] // parts, ids.shape[1]
    groups = queries // GROUP
    share = pl.BlockSpec((queries, slots), lambda i, s: (part, 0))
    held, width = slab.shape
    padded = -(-width // WIDE) * WIDE
    rows = queries * parts // terms
    given = [] if coded is None else [coded]
    span = (terms // parts, rows, images)
    kept = -(-(terms // parts) // 8) * 8
    return pl.pallas_call(
        score_kernel,
        grid_spec=pltpu.PrefetchScalarGridSpec(
            num_scalar_prefetch=1,
            grid=(1,),
            in_specs=[share, share, pl.BlockSpec(memory_space=pltpu.HBM)]
            + [pl.BlockSpec(memory_space=pl.ANY)] * len(given),
            out_specs=[
                pl.BlockSpec((queries, padded), lambda i, s: (0, 0)),
                pl.BlockSpec(span, lambda i, s: (part, 0, 0)),
                pl.BlockSpec((kept, rows), lambda i, s: (0, 0)),
            ],
            scratch_shapes=[
                pltpu.VMEM((rows, images), F32),
                pltpu.VMEM(slab.shape, BF16),
                pltpu.VMEM((queries, slots), F32),
                pltpu.VMEM((groups, GROUP * slots), jnp.int32),
                pltpu.VMEM((groups, GROUP * slots), F32),
                pltpu.SemaphoreType.DMA,
            ],
        ),
        out_shape=[
            pltpu.HBM((queries, padded), BF16),
            pltpu.HBM((terms, rows, images), jnp.int16),
            jax.ShapeDtypeStruct((kept, rows), F32),
        ],
        input_output_aliases={} if coded is None else {4: 1},
        compiler_params=pltpu.CompilerParams(vmem_limit_bytes=VMEM_BYTES),
        cost_estimate=pl.CostEstimate(flops=K1COST, bytes_accessed=1024, transcendentals=0),
        name="score_slab",
    )(place, ids, weights, slab, *given)


def project_kernel(counts, block, images, patches, spans, place, *refs):
    groups = []
    for count in counts:
        groups.append(refs[:count])
        refs = refs[count:]
    features, weights, dense = groups
    bias, running, out, rows, gathered, wide, came_f, came_w, came_d = refs
    depth, columns = weights[0].shape[0], gathered.shape[1]
    index = place[0]

    rows_in = []
    for k, (source, start) in enumerate(zip(weights, spans)):
        at = pl.multiple_of(jnp.bitwise_xor(index, k) * depth, depth)
        rows_in.append(
            pltpu.make_async_copy(
                source.at[:, start : start + columns], gathered.at[pl.ds(at, depth), :], came_w.at[k]
            )
        )
    features_in, at = [], 0
    for k, source in enumerate(features):
        size = source.shape[0]
        copy = pltpu.make_async_copy(source, rows.at[at : at + size], came_f.at[k])
        features_in.append((at, copy))
        at += size
    start, size = spans[0], wide.shape[2]
    dense_in = [
        pltpu.make_async_copy(source.at[:, start : start + size], wide.at[k], came_d.at[k])
        for k, source in enumerate(dense)
    ]
    for copy in rows_in + [copy for _, copy in features_in] + dense_in:
        copy.start()
    for copy in rows_in:
        copy.wait()
    best = None
    for first in range(0, rows.shape[0], block):
        for at, copy in features_in:
            if first <= at < first + block:
                copy.wait()
        held = rows[first : first + block]
        real = held[:, 0:1].astype(F32) < jnp.inf
        tops = []
        for left in range(0, columns, TILE):
            right = min(left + TILE, columns)
            logits = jnp.dot(held, gathered[:, left:right], preferred_element_type=F32)
            logits = jnp.where(real, logits, -jnp.inf)
            logits = logits.reshape(-1, images, patches, right - left)
            tops.append(jnp.max(jnp.max(logits, axis=0), axis=1))
        tops = tops[0] if len(tops) == 1 else jnp.concatenate(tops, axis=1)
        best = tops if best is None else jnp.maximum(best, tops)
    active = jnp.log1p(jnp.maximum(best + bias[...], 0.0))
    pooled = jnp.concatenate([active, jnp.zeros_like(active)], axis=0).astype(BF16)
    queries, lines = out.shape[2], out.shape[1]
    t = 0
    for k, copy in enumerate(dense_in):
        copy.wait()
        found = lax.dot_general(
            pooled, wide[k, :, :columns], ROWS_BY_ROWS, preferred_element_type=F32
        )
        for left in range(0, found.shape[1], queries):
            out[t] = running[t] + found[:lines, left : left + queries]
            t += 1


def project(index, features, weights, spans, bias, dense, running, images, patches):
    width = features[0].shape[1]
    columns = bias.shape[1]
    total = sum(f.shape[0] for f in features)
    block = 512 if total % 512 == 0 else total
    queries, padded = dense[0].shape
    tail = spans[0] + columns >= padded - WIDE + 1 and columns % LANES
    kept = padded - spans[0] if tail else columns
    inputs = [*features, *weights, *dense]
    local = pl.BlockSpec(memory_space=pltpu.VMEM)
    return pl.pallas_call(
        functools.partial(
            project_kernel,
            (len(features), len(weights), len(dense)),
            block,
            images,
            patches,
            spans,
        ),
        in_specs=[pl.BlockSpec(memory_space=pltpu.SMEM)]
        + [pl.BlockSpec(memory_space=pl.ANY)] * len(inputs)
        + [local, local],
        out_specs=local,
        scratch_shapes=[
            pltpu.VMEM((total, width), BF16),
            pltpu.VMEM((width, columns), BF16),
            pltpu.VMEM((len(dense), queries, kept), BF16),
            pltpu.SemaphoreType.DMA((len(features),)),
            pltpu.SemaphoreType.DMA((len(weights),)),
            pltpu.SemaphoreType.DMA((len(dense),)),
        ],
        out_shape=jax.ShapeDtypeStruct(running.shape, F32),
        compiler_params=pltpu.CompilerParams(vmem_limit_bytes=40 << 20),
        cost_estimate=BRIEF,
        name="project",
    )(jnp.stack([index]).astype(jnp.int32), *inputs, bias, running)


def finish_kernel(images, coded, fresh, out, table):
    terms, queries, _ = coded.shape
    total = None
    for t in range(fresh.shape[0]):
        part = fresh[t]
        total = part if total is None else total + part
    table[...] = jnp.zeros(table.shape, F32)
    table[LANES - images :, :queries] = total[:images]
    for t in range(terms):
        table[t : t + 1, :queries] = fresh[t][images : images + 1]
    columns = jnp.swapaxes(table[...], 0, 1)[:queries]
    stored = None
    for t in range(terms):
        part = (coded[t].astype(jnp.int32) + OFFSET).astype(F32) * columns[:, t : t + 1]
        stored = part if stored is None else stored + part
    out[...] = stored
    tail = out.shape[1] - LANES
    lane = lax.broadcasted_iota(jnp.int32, (queries, LANES), 1)
    out[:, tail:] = jnp.where(lane < LANES - images, stored[:, tail:], columns)


def finish(coded, fresh, images):
    _, queries, total = coded.shape
    local = pl.BlockSpec(memory_space=pltpu.VMEM)
    return pl.pallas_call(
        functools.partial(finish_kernel, images),
        in_specs=[local, local],
        out_specs=local,
        scratch_shapes=[pltpu.VMEM((LANES, LANES), F32)],
        out_shape=jax.ShapeDtypeStruct((queries, total), F32),
        compiler_params=pltpu.CompilerParams(vmem_limit_bytes=16 << 20),
        cost_estimate=BRIEF,
        name="finish",
    )(coded, fresh)


def column_blocks(width):
    if width % LANES or width < 8 * LANES:
        return [(0, width)]
    tiles = width // LANES
    small = max(1, tiles * 2 // 15)
    sizes = [tiles * 6 // 30, tiles - tiles * 6 // 30 - small, small]
    return [(sum(sizes[:i]) * LANES, size * LANES) for i, size in enumerate(sizes)]


def shards(rows, terms, patches, patch_mask, proj_weight, proj_bias, slab, query_ids, term_weights):
    along_x = 1
    while along_x * along_x * 4 <= terms:
        along_x *= 2
    along_z = terms // along_x
    row, core, term = lax.axis_index("row"), lax.axis_index("core"), lax.axis_index("term")
    images, patch_rows, features = patches.shape
    width = proj_weight.shape[1]
    held = slab.shape[0]
    block_queries = query_ids.shape[0] // terms

    def to_term(value, k):
        return lax.ppermute(value, "term", [(i, i ^ k) for i in range(terms)])

    def to_row(value, k):
        return lax.ppermute(value, "row", [(i, i ^ k) for i in range(rows)])

    def to_core(value):
        return lax.ppermute(value, "core", [(0, 1), (1, 0)])

    def after(value, *done):
        return lax.optimization_barrier((value, done))[0]

    blocks = column_blocks(width)
    crossed = []
    for b, (start, size) in enumerate(blocks):
        sent = proj_weight[:, start : start + size]
        crossed.append([to_row(sent, k) for k in range(1, rows)])
        if not b:
            patches = after(patches, sent)

    marked = jnp.where(patch_mask[:, :, None] > 0, patches, jnp.array(jnp.inf, BF16))
    marked = marked.reshape(images * patch_rows, features)
    first_x = [to_term(marked, k) for k in range(1, along_x)]
    by_z = [to_term(marked, k * along_x) for k in range(1, along_z)]
    second_x = [[to_term(block, k) for block in by_z] for k in range(1, along_x)]
    gathered = [marked, *by_z, *first_x]
    for blocks_x in second_x:
        gathered += blocks_x

    place = jnp.stack([term * width]).astype(jnp.int32)
    dense, scales, coded = [], [], None
    for part in range(PARTS):
        here = after(place, by_z, first_x, crossed[0]) if part else place
        full, coded, scale = score_slab(
            here, query_ids, term_weights, slab, terms, held + images, part, PARTS, coded
        )
        dense.append(full)
        scales.append(scale[: terms // PARTS])
    coded = after(coded, crossed[:-1], second_x)
    coded = lax.all_to_all(coded, "term", split_axis=0, concat_axis=0, tiled=True)

    scales = jnp.concatenate(scales).reshape(terms, 1, block_queries)
    running = jnp.concatenate(
        [jnp.zeros((terms, images, block_queries), F32), scales,
         jnp.zeros((terms, 7 - images, block_queries), F32)], axis=1)
    bias = proj_bias.reshape(1, width)
    beside = to_core(after(proj_weight, by_z))
    swapped = [[to_core(part) for part in came] for came in crossed]
    for b, (start, size) in enumerate(blocks):
        pieces = [proj_weight, beside]
        for mine, other in zip(crossed[b], swapped[b]):
            pieces += [mine, other]
        if 0 < b < len(blocks) - 1:
            running = after(running, crossed[-1])
        spans = [start, start] + [0] * (len(pieces) - 2)
        running = project(
            2 * row + core, gathered, pieces, spans, bias[:, start : start + size],
            dense, running, images, patch_rows,
        )
    running, coded = lax.optimization_barrier((running, coded))
    fresh = lax.all_to_all(running, "term", split_axis=0, concat_axis=0, tiled=True)
    return finish(coded, fresh, images)


def solution(mesh):
    groups, terms = mesh.shape["img"], mesh.shape["term"]
    rows = groups // 2
    cores = Mesh(mesh.devices.reshape(rows, 2, terms), ("row", "core", "term"))
    img = ("row", "core")
    placed = (
        P(img, "term", None),
        P(img, "term"),
        P(img, "term"),
        P("term"),
        P(img, "term"),
        P(),
        P(),
    )
    return jax.shard_map(
        functools.partial(shards, rows, terms),
        mesh=cores,
        in_specs=placed,
        out_specs=P("term", img),
        check_vma=False,
    )
```

```python
import functools

import jax
import jax.numpy as jnp
from jax import lax
from jax.experimental import pallas as pl
from jax.experimental.pallas import tpu as pltpu
from jax.sharding import Mesh, PartitionSpec as P

BF16 = jnp.bfloat16
F32 = jnp.float32
LANES = 128
WIDE = 256
GROUP = 8
ROWS_BY_ROWS = (((1,), (1,)), ((), ()))
VMEM_BYTES = 61 << 20
LEVELS, OFFSET, TINY = 65535.0, 32768, 1e-30
PARTS = 2
K1COST = 13 << 30
TILE = 768
BRIEF = pl.CostEstimate(flops=1024, bytes_accessed=1024, transcendentals=0)


def whole(array):
    return pl.BlockSpec(array.shape, lambda i, *_: (0,) * array.ndim)


def expand_terms(slots, blocks, width, base, ids, weights, out, row):
    query = lax.broadcasted_iota(jnp.int32, (1, GROUP * slots), 1) // slots
    parts = []
    for g in range(2):
        local = ids[pl.ds(2 * row + g, 1), :] - base
        inside = (local >= 0) & (local < width)
        key = jnp.where(inside, (local // WIDE) * GROUP + query, -1)
        rows = lax.broadcasted_iota(jnp.int32, (blocks * GROUP, GROUP * slots), 0)
        coarse = jnp.where(rows == key, weights[pl.ds(2 * row + g, 1), :], 0.0).astype(BF16)
        place = lax.broadcasted_iota(jnp.int32, (WIDE, GROUP * slots), 0)
        fine = jnp.where(place == (local & (WIDE - 1)), 1.0, 0.0).astype(BF16)
        parts.append(
            lax.dot_general(coarse, fine, ROWS_BY_ROWS, preferred_element_type=F32)
        )
    start = pl.multiple_of(row * 2 * GROUP, 2 * GROUP)
    for b in range(blocks):
        pair = [part[b * GROUP : (b + 1) * GROUP] for part in parts]
        out[pl.ds(start, 2 * GROUP), b * WIDE : (b + 1) * WIDE] = jnp.concatenate(
            pair, axis=0
        ).astype(BF16)


def score_kernel(place, query_ids, term_weights, slab, *refs):
    dense_out, coded, scales, dense, whole_row, stored, listed, weighed, ids, weights, came, sent = refs[-12:]
    slots = query_ids.shape[0]
    images, width = slab.shape
    terms, queries, _ = coded.shape
    blocks = dense.shape[1] // WIDE
    steps = ids.shape[0] // 2
    fetch = pltpu.make_async_copy(slab, stored, came)
    fetch.start()
    given = term_weights[...].astype(F32)
    listed[...] = jnp.swapaxes(query_ids[...], 0, 1)
    weighed[...] = jnp.swapaxes(jnp.where(query_ids[...] >= 0, given, 0.0), 0, 1)
    for q in range(GROUP):
        rows = pl.ds(q, ids.shape[0], stride=GROUP)
        ids[:, q * slots : (q + 1) * slots] = listed[rows, :]
        weights[:, q * slots : (q + 1) * slots] = weighed[rows, :]

    def step(row, carry):
        expand_terms(slots, blocks, width, place[0], ids, weights, dense, row)
        return carry

    shares = 4 if steps % 4 == 0 else 1
    count = steps // shares
    leaving = []
    for share in range(shares):
        lax.fori_loop(
            share * count, (share + 1) * count, step, 0, unroll=8 if count % 8 == 0 else 1
        )
        done = pl.ds(share * count * 2 * GROUP, count * 2 * GROUP)
        leaving.append(pltpu.make_async_copy(dense.at[done], dense_out.at[done], sent.at[share]))
        leaving[-1].start()
    fetch.wait()
    found = lax.dot_general(
        dense[:, :width], stored[...], ROWS_BY_ROWS, preferred_element_type=F32
    )
    lane = lax.broadcasted_iota(jnp.int32, (queries, LANES), 1)
    tops = jnp.zeros((queries, LANES), F32)
    whole_row[...] = jnp.zeros(whole_row.shape, F32)
    for t in range(terms):
        part = found[t * queries : (t + 1) * queries]
        top = jnp.maximum(jnp.max(part, axis=1, keepdims=True), TINY)
        whole_row[:, :images] = part * (LEVELS / top) + 0.5
        coded[t] = (whole_row[...].astype(jnp.int32) - OFFSET).astype(jnp.int16)
        tops = jnp.where(lane == t, top * (1.0 / LEVELS), tops)
    scales[...] = jnp.swapaxes(tops, 0, 1)[: scales.shape[0]]
    for copy in leaving:
        copy.wait()


def score_slab(place, ids, weights, slab, terms, images, part, parts, coded):
    slots, queries = ids.shape[0], ids.shape[1] // parts
    groups = queries // GROUP
    share = pl.BlockSpec((slots, queries), lambda i, s: (0, part))
    held, width = slab.shape
    padded = -(-width // WIDE) * WIDE
    rows = queries * parts // terms
    given = [] if coded is None else [coded]
    span = (terms // parts, rows, images)
    kept = -(-(terms // parts) // 8) * 8
    return pl.pallas_call(
        score_kernel,
        grid_spec=pltpu.PrefetchScalarGridSpec(
            num_scalar_prefetch=1,
            grid=(1,),
            in_specs=[share, share, pl.BlockSpec(memory_space=pltpu.HBM)]
            + [pl.BlockSpec(memory_space=pl.ANY)] * len(given),
            out_specs=[
                pl.BlockSpec(memory_space=pl.ANY),
                pl.BlockSpec(span, lambda i, s: (part, 0, 0)),
                pl.BlockSpec((kept, rows), lambda i, s: (0, 0)),
            ],
            scratch_shapes=[
                pltpu.VMEM((queries, padded), BF16),
                pltpu.VMEM((rows, images), F32),
                pltpu.VMEM(slab.shape, BF16),
                pltpu.VMEM((queries, slots), jnp.int32),
                pltpu.VMEM((queries, slots), F32),
                pltpu.VMEM((groups, GROUP * slots), jnp.int32),
                pltpu.VMEM((groups, GROUP * slots), F32),
                pltpu.SemaphoreType.DMA,
                pltpu.SemaphoreType.DMA((4,)),
            ],
        ),
        out_shape=[
            pltpu.HBM((queries, padded), BF16),
            pltpu.HBM((terms, rows, images), jnp.int16),
            jax.ShapeDtypeStruct((kept, rows), F32),
        ],
        input_output_aliases={} if coded is None else {4: 1},
        compiler_params=pltpu.CompilerParams(vmem_limit_bytes=44 << 20),
        cost_estimate=pl.CostEstimate(flops=K1COST, bytes_accessed=1024, transcendentals=0),
        name="score_slab",
    )(place, ids, weights, pltpu.with_memory_space_constraint(slab, pltpu.HBM), *given)


def project_kernel(counts, block, images, patches, spans, offset, place, *refs):
    groups = []
    for count in counts:
        groups.append(refs[:count])
        refs = refs[count:]
    features, weights, dense = groups
    bias, running, out, rows, gathered, wide, came_f, came_w, came_d = refs
    depth, columns = weights[0].shape[0], gathered.shape[1]
    index = place[0]

    tiles = [(left, min(left + TILE, columns)) for left in range(0, columns, TILE)]
    if columns % LANES:
        tiles = [(0, columns)]

    def fetch_rows(j, k):
        left, right = tiles[j]
        at = pl.multiple_of(jnp.bitwise_xor(index, k) * depth, depth)
        return pltpu.make_async_copy(
            weights[k].at[:, spans[k] + left : spans[k] + right],
            gathered.at[pl.ds(at, depth), left:right],
            came_w.at[j, k],
        )

    def fetch_dense(j, k):
        left, right = tiles[j]
        if columns % LANES:
            return pltpu.make_async_copy(dense[k], wide.at[k], came_d.at[j, k])
        return pltpu.make_async_copy(
            dense[k].at[:, offset + left : offset + right],
            wide.at[k, :, left:right],
            came_d.at[j, k],
        )

    for k in range(len(weights)):
        fetch_rows(0, k).start()
    features_in, at = [], 0
    for k, source in enumerate(features):
        size = source.shape[0]
        copy = pltpu.make_async_copy(source, rows.at[at : at + size], came_f.at[k])
        copy.start()
        features_in.append((at, copy))
        at += size
    for j in range(len(tiles)):
        if j:
            for k in range(len(weights)):
                fetch_rows(j, k).start()
        for k in range(len(dense)):
            fetch_dense(j, k).start()
    queries, lines = out.shape[2], out.shape[1]
    sums = [None] * len(dense)
    for j, (left, right) in enumerate(tiles):
        for k in range(len(weights)):
            fetch_rows(j, k).wait()
        best = None
        for first in range(0, rows.shape[0], block):
            for at, copy in features_in:
                if not j and first <= at < first + block:
                    copy.wait()
            held = rows[first : first + block]
            real = held[:, 0:1].astype(F32) < jnp.inf
            logits = jnp.dot(held, gathered[:, left:right], preferred_element_type=F32)
            logits = jnp.where(real, logits, -jnp.inf)
            logits = logits.reshape(-1, images, patches, right - left)
            tops = jnp.max(jnp.max(logits, axis=0), axis=1)
            best = tops if best is None else jnp.maximum(best, tops)
        active = jnp.log1p(jnp.maximum(best + bias[:, left:right], 0.0))
        pooled = jnp.concatenate([active, jnp.zeros_like(active)], axis=0).astype(BF16)
        for k in range(len(dense)):
            fetch_dense(j, k).wait()
            part = lax.dot_general(
                pooled, wide[k, :, left:right], ROWS_BY_ROWS, preferred_element_type=F32
            )
            sums[k] = part if sums[k] is None else sums[k] + part
    t = 0
    for found in sums:
        for left in range(0, found.shape[1], queries):
            out[t] = running[t] + found[:lines, left : left + queries]
            t += 1


def project(index, features, weights, spans, offset, bias, dense, running, images, patches):
    width = features[0].shape[1]
    columns = bias.shape[1]
    total = sum(f.shape[0] for f in features)
    block = 512 if total % 512 == 0 else total
    queries, padded = dense[0].shape
    tail = offset + columns >= padded - WIDE + 1 and columns % LANES
    kept = padded - offset if tail else columns
    inputs = [*features, *weights, *dense]
    local = pl.BlockSpec(memory_space=pltpu.VMEM)
    return pl.pallas_call(
        functools.partial(
            project_kernel,
            (len(features), len(weights), len(dense)),
            block,
            images,
            patches,
            spans,
            offset,
        ),
        in_specs=[pl.BlockSpec(memory_space=pltpu.SMEM)]
        + [pl.BlockSpec(memory_space=pl.ANY)] * len(inputs)
        + [local, local],
        out_specs=local,
        scratch_shapes=[
            pltpu.VMEM((total, width), BF16),
            pltpu.VMEM((width, columns), BF16),
            pltpu.VMEM((len(dense), queries, kept), BF16),
            pltpu.SemaphoreType.DMA((len(features),)),
            pltpu.SemaphoreType.DMA((-(-columns // TILE), len(weights))),
            pltpu.SemaphoreType.DMA((-(-columns // TILE), len(dense))),
        ],
        out_shape=jax.ShapeDtypeStruct(running.shape, F32),
        compiler_params=pltpu.CompilerParams(vmem_limit_bytes=40 << 20),
        cost_estimate=BRIEF,
        name="project",
    )(
        jnp.stack([index]).astype(jnp.int32),
        *[pltpu.with_memory_space_constraint(f, pltpu.HBM) for f in features],
        *weights,
        *dense,
        bias,
        running,
    )


def finish_kernel(images, coded, fresh, out, table):
    terms, queries, _ = coded.shape
    total = None
    for t in range(fresh.shape[0]):
        part = fresh[t]
        total = part if total is None else total + part
    table[...] = jnp.zeros(table.shape, F32)
    table[LANES - images :, :queries] = total[:images]
    for t in range(terms):
        table[t : t + 1, :queries] = fresh[t][images : images + 1]
    columns = jnp.swapaxes(table[...], 0, 1)[:queries]
    stored = None
    for t in range(terms):
        part = (coded[t].astype(jnp.int32) + OFFSET).astype(F32) * columns[:, t : t + 1]
        stored = part if stored is None else stored + part
    out[...] = stored
    tail = out.shape[1] - LANES
    lane = lax.broadcasted_iota(jnp.int32, (queries, LANES), 1)
    out[:, tail:] = jnp.where(lane < LANES - images, stored[:, tail:], columns)


def finish(coded, fresh, images):
    _, queries, total = coded.shape
    local = pl.BlockSpec(memory_space=pltpu.VMEM)
    return pl.pallas_call(
        functools.partial(finish_kernel, images),
        in_specs=[local, local],
        out_specs=local,
        scratch_shapes=[pltpu.VMEM((LANES, LANES), F32)],
        out_shape=jax.ShapeDtypeStruct((queries, total), F32),
        compiler_params=pltpu.CompilerParams(vmem_limit_bytes=16 << 20),
        cost_estimate=BRIEF,
        name="finish",
    )(coded, fresh)


def column_blocks(width):
    if width % LANES or width < 8 * LANES:
        return [(0, width)]
    tiles = width // LANES
    small = max(1, tiles * 2 // 15)
    sizes = [tiles * 9 // 30, tiles - tiles * 9 // 30 - small, small]
    return [(sum(sizes[:i]) * LANES, size * LANES) for i, size in enumerate(sizes)]


def shards(rows, terms, patches, patch_mask, proj_weight, proj_bias, slab, query_ids, term_weights):
    along_x = 1
    while along_x * along_x * 4 <= terms:
        along_x *= 2
    along_z = terms // along_x
    row, core, term = lax.axis_index("row"), lax.axis_index("core"), lax.axis_index("term")
    images, patch_rows, features = patches.shape
    width = proj_weight.shape[1]
    held = slab.shape[0]
    block_queries = query_ids.shape[0] // terms

    def to_term(value, k):
        return lax.ppermute(value, "term", [(i, i ^ k) for i in range(terms)])

    def to_row(value, k):
        return lax.ppermute(value, "row", [(i, i ^ k) for i in range(rows)])

    def to_core(value):
        return lax.ppermute(value, "core", [(0, 1), (1, 0)])

    def after(value, *done):
        return lax.optimization_barrier((value, done))[0]

    blocks = column_blocks(width)
    crossed, local = [], []
    for b, (start, size) in enumerate(blocks):
        sent = proj_weight[:, start : start + size]
        local.append(sent)
        crossed.append([to_row(sent, k) for k in range(1, rows)])
        if not b:
            patches = after(patches, sent)

    marked = jnp.where(patch_mask[:, :, None] > 0, patches, jnp.array(jnp.inf, BF16))
    marked = marked.reshape(images * patch_rows, features)
    first_x = [to_term(marked, k) for k in range(1, along_x)]
    by_z = []
    for k in range(1, along_z):
        near = k & -k
        by_z.append(to_term(by_z[k - near - 1] if k > near else marked, near * along_x))
    second_x = [[to_term(block, k) for block in by_z] for k in range(1, along_x)]
    gathered = [marked, *by_z, *first_x]
    for blocks_x in second_x:
        gathered += blocks_x

    place = jnp.stack([term * width]).astype(jnp.int32)
    dense, scales, coded = [], [], None
    for part in range(PARTS):
        here = after(place, by_z[:1], first_x, [v[:1] for v in second_x], local[-1]) if part else place
        full, coded, scale = score_slab(
            here, query_ids.T, term_weights.T, slab, terms, held + images, part, PARTS, coded
        )
        dense.append(pltpu.with_memory_space_constraint(full, pltpu.HBM))
        scales.append(scale[: terms // PARTS])
    coded = after(coded, crossed[:1], second_x)
    coded = lax.all_to_all(coded, "term", split_axis=0, concat_axis=0, tiled=True)

    scales = jnp.concatenate(scales).reshape(terms, 1, block_queries)
    running = jnp.concatenate(
        [jnp.zeros((terms, images, block_queries), F32), scales,
         jnp.zeros((terms, 7 - images, block_queries), F32)], axis=1)
    bias = proj_bias.reshape(1, width)
    beside = to_core(after(proj_weight, by_z))
    for b, (start, size) in enumerate(blocks):
        if not b or b < len(blocks) - 1:
            swapped = [to_core(part) for part in crossed[b]]
        pieces = [local[b], beside]
        for mine, other in zip(crossed[b], swapped):
            pieces += [mine, other]
        spans = [0, start] + [0] * (len(pieces) - 2)
        running = project(
            2 * row + core, gathered, pieces, spans, start, bias[:, start : start + size],
            dense, running, images, patch_rows,
        )
        if b == len(blocks) - 3:
            swapped_last = [to_core(part) for part in after(crossed[-1], running)]
            running = after(running, crossed[-1])
        if b == len(blocks) - 2:
            swapped = swapped_last
    running, coded = lax.optimization_barrier((running, coded))
    fresh = lax.all_to_all(running, "term", split_axis=0, concat_axis=0, tiled=True)
    return finish(coded, fresh, images)


def solution(mesh):
    groups, terms = mesh.shape["img"], mesh.shape["term"]
    rows = groups // 2
    cores = Mesh(mesh.devices.reshape(rows, 2, terms), ("row", "core", "term"))
    img = ("row", "core")
    placed = (
        P(img, "term", None),
        P(img, "term"),
        P(img, "term"),
        P("term"),
        P(img, "term"),
        P(),
        P(),
    )
    return jax.shard_map(
        functools.partial(shards, rows, terms),
        mesh=cores,
        in_specs=placed,
        out_specs=P("term", img),
        check_vma=False,
    )
```

```python
import functools

import jax
import jax.numpy as jnp
from jax import lax
from jax.experimental import pallas as pl
from jax.experimental.pallas import tpu as pltpu
from jax.sharding import Mesh, PartitionSpec as P

BF16 = jnp.bfloat16
F32 = jnp.float32
LANES = 128
WIDE = 256
GROUP = 8
ROWS_BY_ROWS = (((1,), (1,)), ((), ()))
VMEM_BYTES = 61 << 20
LEVELS, OFFSET, TINY = 65535.0, 32768, 1e-30
PARTS = 2
K1COST = 13 << 30
TILE = 1152
BRIEF = pl.CostEstimate(flops=1024, bytes_accessed=1024, transcendentals=0)


def whole(array):
    return pl.BlockSpec(array.shape, lambda i, *_: (0,) * array.ndim)


def expand_terms(slots, blocks, width, base, ids, weights, out, row):
    query = lax.broadcasted_iota(jnp.int32, (1, GROUP * slots), 1) // slots
    parts = []
    for g in range(2):
        local = ids[pl.ds(2 * row + g, 1), :] - base
        inside = (local >= 0) & (local < width)
        key = jnp.where(inside, (local // WIDE) * GROUP + query, -1)
        rows = lax.broadcasted_iota(jnp.int32, (blocks * GROUP, GROUP * slots), 0)
        coarse = jnp.where(rows == key, weights[pl.ds(2 * row + g, 1), :], 0.0).astype(BF16)
        place = lax.broadcasted_iota(jnp.int32, (WIDE, GROUP * slots), 0)
        fine = jnp.where(place == (local & (WIDE - 1)), 1.0, 0.0).astype(BF16)
        parts.append(
            lax.dot_general(coarse, fine, ROWS_BY_ROWS, preferred_element_type=F32)
        )
    start = pl.multiple_of(row * 2 * GROUP, 2 * GROUP)
    for b in range(blocks):
        pair = [part[b * GROUP : (b + 1) * GROUP] for part in parts]
        out[pl.ds(start, 2 * GROUP), b * WIDE : (b + 1) * WIDE] = jnp.concatenate(
            pair, axis=0
        ).astype(BF16)


def score_kernel(place, query_ids, term_weights, slab, *refs):
    dense_out, coded, scales, dense, whole_row, stored, listed, weighed, ids, weights, came, sent = refs[-12:]
    slots = query_ids.shape[0]
    images, width = slab.shape
    terms, queries, _ = coded.shape
    blocks = dense.shape[1] // WIDE
    steps = ids.shape[0] // 2
    fetch = pltpu.make_async_copy(slab, stored, came)
    fetch.start()
    given = term_weights[...].astype(F32)
    listed[...] = jnp.swapaxes(query_ids[...], 0, 1)
    weighed[...] = jnp.swapaxes(jnp.where(query_ids[...] >= 0, given, 0.0), 0, 1)
    for q in range(GROUP):
        rows = pl.ds(q, ids.shape[0], stride=GROUP)
        ids[:, q * slots : (q + 1) * slots] = listed[rows, :]
        weights[:, q * slots : (q + 1) * slots] = weighed[rows, :]

    def step(row, carry):
        expand_terms(slots, blocks, width, place[0], ids, weights, dense, row)
        return carry

    shares = 4 if steps % 4 == 0 else 1
    count = steps // shares
    leaving = []
    for share in range(shares):
        lax.fori_loop(
            share * count, (share + 1) * count, step, 0, unroll=8 if count % 8 == 0 else 1
        )
        done = pl.ds(share * count * 2 * GROUP, count * 2 * GROUP)
        leaving.append(pltpu.make_async_copy(dense.at[done], dense_out.at[done], sent.at[share]))
        leaving[-1].start()
    fetch.wait()
    found = lax.dot_general(
        dense[:, :width], stored[...], ROWS_BY_ROWS, preferred_element_type=F32
    )
    lane = lax.broadcasted_iota(jnp.int32, (queries, LANES), 1)
    tops = jnp.zeros((queries, LANES), F32)
    whole_row[...] = jnp.zeros(whole_row.shape, F32)
    for t in range(terms):
        part = found[t * queries : (t + 1) * queries]
        top = jnp.maximum(jnp.max(part, axis=1, keepdims=True), TINY)
        whole_row[:, :images] = part * (LEVELS / top) + 0.5
        coded[t] = (whole_row[...].astype(jnp.int32) - OFFSET).astype(jnp.int16)
        tops = jnp.where(lane == t, top * (1.0 / LEVELS), tops)
    scales[...] = jnp.swapaxes(tops, 0, 1)[: scales.shape[0]]
    for copy in leaving:
        copy.wait()


def score_slab(place, ids, weights, slab, terms, images, part, parts, coded):
    slots, queries = ids.shape[0], ids.shape[1] // parts
    groups = queries // GROUP
    share = pl.BlockSpec((slots, queries), lambda i, s: (0, part))
    held, width = slab.shape
    padded = -(-width // WIDE) * WIDE
    rows = queries * parts // terms
    given = [] if coded is None else [coded]
    span = (terms // parts, rows, images)
    kept = -(-(terms // parts) // 8) * 8
    return pl.pallas_call(
        score_kernel,
        grid_spec=pltpu.PrefetchScalarGridSpec(
            num_scalar_prefetch=1,
            grid=(1,),
            in_specs=[share, share, pl.BlockSpec(memory_space=pltpu.HBM)]
            + [pl.BlockSpec(memory_space=pl.ANY)] * len(given),
            out_specs=[
                pl.BlockSpec(memory_space=pl.ANY),
                pl.BlockSpec(span, lambda i, s: (part, 0, 0)),
                pl.BlockSpec((kept, rows), lambda i, s: (0, 0)),
            ],
            scratch_shapes=[
                pltpu.VMEM((queries, padded), BF16),
                pltpu.VMEM((rows, images), F32),
                pltpu.VMEM(slab.shape, BF16),
                pltpu.VMEM((queries, slots), jnp.int32),
                pltpu.VMEM((queries, slots), F32),
                pltpu.VMEM((groups, GROUP * slots), jnp.int32),
                pltpu.VMEM((groups, GROUP * slots), F32),
                pltpu.SemaphoreType.DMA,
                pltpu.SemaphoreType.DMA((4,)),
            ],
        ),
        out_shape=[
            pltpu.HBM((queries, padded), BF16),
            pltpu.HBM((terms, rows, images), jnp.int16),
            jax.ShapeDtypeStruct((kept, rows), F32),
        ],
        input_output_aliases={} if coded is None else {4: 1},
        compiler_params=pltpu.CompilerParams(vmem_limit_bytes=44 << 20),
        cost_estimate=pl.CostEstimate(flops=K1COST, bytes_accessed=1024, transcendentals=0),
        name="score_slab",
    )(place, ids, weights, pltpu.with_memory_space_constraint(slab, pltpu.HBM), *given)


def project_kernel(counts, block, images, patches, spans, offset, place, *refs):
    groups = []
    for count in counts:
        groups.append(refs[:count])
        refs = refs[count:]
    features, weights, dense = groups
    bias, running, out, rows, gathered, wide, came_f, came_w, came_d = refs
    depth, columns = weights[0].shape[0], gathered.shape[1]
    index = place[0]

    tiles = [(left, min(left + TILE, columns)) for left in range(0, columns, TILE)]
    if columns % LANES:
        tiles = [(0, columns)]

    def fetch_rows(j, k):
        left, right = tiles[j]
        at = pl.multiple_of(jnp.bitwise_xor(index, k) * depth, depth)
        return pltpu.make_async_copy(
            weights[k].at[:, spans[k] + left : spans[k] + right],
            gathered.at[pl.ds(at, depth), left:right],
            came_w.at[j, k],
        )

    def fetch_dense(j, k):
        left, right = tiles[j]
        if columns % LANES:
            return pltpu.make_async_copy(dense[k], wide.at[k], came_d.at[j, k])
        return pltpu.make_async_copy(
            dense[k].at[:, offset + left : offset + right],
            wide.at[k, :, left:right],
            came_d.at[j, k],
        )

    def start_features(first):
        for at, copy in features_in:
            if first <= at < first + block:
                copy.start()

    features_in, at = [], 0
    for k, source in enumerate(features):
        size = source.shape[0]
        copy = pltpu.make_async_copy(source, rows.at[at : at + size], came_f.at[k])
        features_in.append((at, copy))
        at += size
    for k in range(len(weights)):
        fetch_rows(0, k).start()
    start_features(0)
    queries, lines = out.shape[2], out.shape[1]
    sums = [None] * len(dense)

    def score(j, pooled):
        left, right = tiles[j]
        for k in range(len(dense)):
            part = lax.dot_general(
                pooled, wide[k, :, left:right], ROWS_BY_ROWS, preferred_element_type=F32
            )
            sums[k] = part if sums[k] is None else sums[k] + part

    pooled = None
    for j, (left, right) in enumerate(tiles):
        for k in range(len(weights)):
            fetch_rows(j, k).wait()
        if j:
            for k in range(len(dense)):
                fetch_dense(j - 1, k).wait()
        best = None
        for first in range(0, rows.shape[0], block):
            for at, copy in features_in:
                if not j and first <= at < first + block:
                    copy.wait()
            if not first:
                if not j:
                    for later in range(block, rows.shape[0], block):
                        start_features(later)
                    for k in range(len(dense)):
                        fetch_dense(0, k).start()
                if j + 1 < len(tiles):
                    for k in range(len(weights)):
                        fetch_rows(j + 1, k).start()
                    for k in range(len(dense)):
                        fetch_dense(j + 1, k).start()
            held = rows[first : first + block]
            real = held[:, 0:1].astype(F32) < jnp.inf
            logits = jnp.dot(held, gathered[:, left:right], preferred_element_type=F32)
            if j and not first:
                score(j - 1, pooled)
            logits = jnp.where(real, logits, -jnp.inf)
            logits = logits.reshape(-1, images, patches, right - left)
            tops = jnp.max(jnp.max(logits, axis=0), axis=1)
            best = tops if best is None else jnp.maximum(best, tops)
        active = jnp.log1p(jnp.maximum(best + bias[:, left:right], 0.0))
        pooled = jnp.concatenate([active, jnp.zeros_like(active)], axis=0).astype(BF16)
    for k in range(len(dense)):
        fetch_dense(len(tiles) - 1, k).wait()
    score(len(tiles) - 1, pooled)
    t = 0
    for found in sums:
        for left in range(0, found.shape[1], queries):
            out[t] = running[t] + found[:lines, left : left + queries]
            t += 1


def project(index, features, weights, spans, offset, bias, dense, running, images, patches):
    width = features[0].shape[1]
    columns = bias.shape[1]
    total = sum(f.shape[0] for f in features)
    block = 512 if total % 512 == 0 else total
    queries, padded = dense[0].shape
    tail = offset + columns >= padded - WIDE + 1 and columns % LANES
    kept = padded - offset if tail else columns
    inputs = [*features, *weights, *dense]
    local = pl.BlockSpec(memory_space=pltpu.VMEM)
    return pl.pallas_call(
        functools.partial(
            project_kernel,
            (len(features), len(weights), len(dense)),
            block,
            images,
            patches,
            spans,
            offset,
        ),
        in_specs=[pl.BlockSpec(memory_space=pltpu.SMEM)]
        + [pl.BlockSpec(memory_space=pl.ANY)] * len(inputs)
        + [local, local],
        out_specs=local,
        scratch_shapes=[
            pltpu.VMEM((total, width), BF16),
            pltpu.VMEM((width, columns), BF16),
            pltpu.VMEM((len(dense), queries, kept), BF16),
            pltpu.SemaphoreType.DMA((len(features),)),
            pltpu.SemaphoreType.DMA((-(-columns // TILE), len(weights))),
            pltpu.SemaphoreType.DMA((-(-columns // TILE), len(dense))),
        ],
        out_shape=jax.ShapeDtypeStruct(running.shape, F32),
        compiler_params=pltpu.CompilerParams(vmem_limit_bytes=40 << 20),
        cost_estimate=BRIEF,
        name="project",
    )(
        jnp.stack([index]).astype(jnp.int32),
        *[pltpu.with_memory_space_constraint(f, pltpu.HBM) for f in features],
        *weights,
        *dense,
        bias,
        running,
    )


def finish_kernel(images, coded, fresh, out, table, held, came):
    terms, queries, _ = coded.shape
    copies = [pltpu.make_async_copy(coded.at[t], held.at[t], came.at[t]) for t in range(terms)]
    for copy in copies:
        copy.start()
    total = None
    for t in range(fresh.shape[0]):
        part = fresh[t]
        total = part if total is None else total + part
    table[...] = jnp.zeros(table.shape, F32)
    table[LANES - images :, :queries] = total[:images]
    for t in range(terms):
        table[t : t + 1, :queries] = fresh[t][images : images + 1]
    columns = jnp.swapaxes(table[...], 0, 1)[:queries]
    stored = None
    for t in range(terms):
        copies[t].wait()
        part = (held[t].astype(jnp.int32) + OFFSET).astype(F32) * columns[:, t : t + 1]
        stored = part if stored is None else stored + part
    out[...] = stored
    tail = out.shape[1] - LANES
    lane = lax.broadcasted_iota(jnp.int32, (queries, LANES), 1)
    out[:, tail:] = jnp.where(lane < LANES - images, stored[:, tail:], columns)


def finish(coded, fresh, images):
    terms, queries, total = coded.shape
    local = pl.BlockSpec(memory_space=pltpu.VMEM)
    return pl.pallas_call(
        functools.partial(finish_kernel, images),
        in_specs=[pl.BlockSpec(memory_space=pl.ANY), local],
        out_specs=local,
        scratch_shapes=[
            pltpu.VMEM((LANES, LANES), F32),
            pltpu.VMEM(coded.shape, jnp.int16),
            pltpu.SemaphoreType.DMA((terms,)),
        ],
        out_shape=jax.ShapeDtypeStruct((queries, total), F32),
        compiler_params=pltpu.CompilerParams(vmem_limit_bytes=16 << 20),
        cost_estimate=BRIEF,
        name="finish",
    )(coded, fresh)


def column_blocks(width):
    if width % LANES or width < 8 * LANES:
        return [(0, width)]
    tiles = width // LANES
    small = max(1, tiles * 2 // 15)
    sizes = [tiles * 9 // 30, tiles - tiles * 9 // 30 - small, small]
    return [(sum(sizes[:i]) * LANES, size * LANES) for i, size in enumerate(sizes)]


def shards(rows, terms, patches, patch_mask, proj_weight, proj_bias, slab, query_ids, term_weights):
    along_x = 1
    while along_x * along_x * 4 <= terms:
        along_x *= 2
    along_z = terms // along_x
    row, core, term = lax.axis_index("row"), lax.axis_index("core"), lax.axis_index("term")
    images, patch_rows, features = patches.shape
    width = proj_weight.shape[1]
    held = slab.shape[0]
    block_queries = query_ids.shape[0] // terms

    def to_term(value, k):
        return lax.ppermute(value, "term", [(i, i ^ k) for i in range(terms)])

    def to_row(value, k):
        return lax.ppermute(value, "row", [(i, i ^ k) for i in range(rows)])

    def to_core(value):
        return lax.ppermute(value, "core", [(0, 1), (1, 0)])

    def after(value, *done):
        return lax.optimization_barrier((value, done))[0]

    blocks = column_blocks(width)
    crossed, local = [], []
    for b, (start, size) in enumerate(blocks):
        sent = proj_weight[:, start : start + size]
        local.append(sent)
        crossed.append([to_row(sent, k) for k in range(1, rows)])
        if not b:
            patches = after(patches, sent)

    marked = jnp.where(patch_mask[:, :, None] > 0, patches, jnp.array(jnp.inf, BF16))
    marked = marked.reshape(images * patch_rows, features)
    first_x = [to_term(marked, k) for k in range(1, along_x)]
    by_z = []
    for k in range(1, along_z):
        near = k & -k
        by_z.append(to_term(by_z[k - near - 1] if k > near else marked, near * along_x))
    second_x = [[to_term(block, k) for block in by_z] for k in range(1, along_x)]
    gathered = [marked, *by_z, *first_x]
    for blocks_x in second_x:
        gathered += blocks_x

    place = jnp.stack([term * width]).astype(jnp.int32)
    dense, scales, coded = [], [], None
    for part in range(PARTS):
        here = after(place, by_z[:1], first_x, [v[:1] for v in second_x], local[-1]) if part else place
        full, coded, scale = score_slab(
            here, query_ids.T, term_weights.T, slab, terms, held + images, part, PARTS, coded
        )
        dense.append(pltpu.with_memory_space_constraint(full, pltpu.HBM))
        scales.append(scale[: terms // PARTS])
    coded = after(coded, crossed[:1], second_x)
    coded = lax.all_to_all(coded, "term", split_axis=0, concat_axis=0, tiled=True)

    scales = jnp.concatenate(scales).reshape(terms, 1, block_queries)
    running = jnp.concatenate(
        [jnp.zeros((terms, images, block_queries), F32), scales,
         jnp.zeros((terms, 7 - images, block_queries), F32)], axis=1)
    bias = proj_bias.reshape(1, width)
    beside = to_core(after(proj_weight, by_z))
    for b, (start, size) in enumerate(blocks):
        if not b or b < len(blocks) - 1:
            swapped = [to_core(part) for part in crossed[b]]
        pieces = [local[b], beside]
        for mine, other in zip(crossed[b], swapped):
            pieces += [mine, other]
        spans = [0, start] + [0] * (len(pieces) - 2)
        running = project(
            2 * row + core, gathered, pieces, spans, start, bias[:, start : start + size],
            dense, running, images, patch_rows,
        )
        if b == len(blocks) - 3:
            swapped_last = [to_core(part) for part in after(crossed[-1], running)]
            running = after(running, crossed[-1])
        if b == len(blocks) - 2:
            swapped = swapped_last
    running, coded = lax.optimization_barrier((running, coded))
    fresh = lax.all_to_all(running, "term", split_axis=0, concat_axis=0, tiled=True)
    return finish(coded, fresh, images)


def solution(mesh):
    groups, terms = mesh.shape["img"], mesh.shape["term"]
    rows = groups // 2
    cores = Mesh(mesh.devices.reshape(rows, 2, terms), ("row", "core", "term"))
    img = ("row", "core")
    placed = (
        P(img, "term", None),
        P(img, "term"),
        P(img, "term"),
        P("term"),
        P(img, "term"),
        P(),
        P(),
    )
    return jax.shard_map(
        functools.partial(shards, rows, terms),
        mesh=cores,
        in_specs=placed,
        out_specs=P("term", img),
        check_vma=False,
    )
```

```python
import functools

import jax
import jax.numpy as jnp
from jax import lax
from jax.experimental import pallas as pl
from jax.experimental.pallas import tpu as pltpu
from jax.sharding import Mesh, PartitionSpec as P

BF16 = jnp.bfloat16
F32 = jnp.float32
LANES = 128
WIDE = 256
GROUP = 8
ROWS_BY_ROWS = (((1,), (1,)), ((), ()))
VMEM_BYTES = 61 << 20
LEVELS, OFFSET, TINY = 65535.0, 32768, 1e-30
PARTS = 2
K1COST = 13 << 30
TILE = 1152
BRIEF = pl.CostEstimate(flops=1024, bytes_accessed=1024, transcendentals=0)


def whole(array):
    return pl.BlockSpec(array.shape, lambda i, *_: (0,) * array.ndim)


def expand_terms(slots, blocks, width, base, ids, weights, out, row):
    query = lax.broadcasted_iota(jnp.int32, (1, GROUP * slots), 1) // slots
    parts = []
    for g in range(2):
        local = ids[pl.ds(2 * row + g, 1), :] - base
        inside = (local >= 0) & (local < width)
        key = jnp.where(inside, (local // WIDE) * GROUP + query, -1)
        rows = lax.broadcasted_iota(jnp.int32, (blocks * GROUP, GROUP * slots), 0)
        coarse = jnp.where(rows == key, weights[pl.ds(2 * row + g, 1), :], 0.0).astype(BF16)
        place = lax.broadcasted_iota(jnp.int32, (WIDE, GROUP * slots), 0)
        fine = jnp.where(place == (local & (WIDE - 1)), 1.0, 0.0).astype(BF16)
        parts.append(
            lax.dot_general(coarse, fine, ROWS_BY_ROWS, preferred_element_type=F32)
        )
    start = pl.multiple_of(row * 2 * GROUP, 2 * GROUP)
    for b in range(blocks):
        pair = [part[b * GROUP : (b + 1) * GROUP] for part in parts]
        out[pl.ds(start, 2 * GROUP), b * WIDE : (b + 1) * WIDE] = jnp.concatenate(
            pair, axis=0
        ).astype(BF16)


def score_kernel(place, query_ids, term_weights, slab, *refs):
    dense_out, coded, scales, dense, whole_row, stored, listed, weighed, ids, weights, came, sent = refs[-12:]
    slots = query_ids.shape[0]
    images, width = slab.shape
    terms, queries, _ = coded.shape
    blocks = dense.shape[1] // WIDE
    steps = ids.shape[0] // 2
    fetch = pltpu.make_async_copy(slab, stored, came)
    fetch.start()
    given = term_weights[...].astype(F32)
    listed[...] = jnp.swapaxes(query_ids[...], 0, 1)
    weighed[...] = jnp.swapaxes(jnp.where(query_ids[...] >= 0, given, 0.0), 0, 1)
    for q in range(GROUP):
        rows = pl.ds(q, ids.shape[0], stride=GROUP)
        ids[:, q * slots : (q + 1) * slots] = listed[rows, :]
        weights[:, q * slots : (q + 1) * slots] = weighed[rows, :]

    def step(row, carry):
        expand_terms(slots, blocks, width, place[0], ids, weights, dense, row)
        return carry

    shares = 4 if steps % 4 == 0 else 1
    count = steps // shares
    leaving = []
    for share in range(shares):
        lax.fori_loop(
            share * count, (share + 1) * count, step, 0, unroll=8 if count % 8 == 0 else 1
        )
        done = pl.ds(share * count * 2 * GROUP, count * 2 * GROUP)
        leaving.append(pltpu.make_async_copy(dense.at[done], dense_out.at[done], sent.at[share]))
        leaving[-1].start()
    fetch.wait()
    found = lax.dot_general(
        dense[:, :width], stored[...], ROWS_BY_ROWS, preferred_element_type=F32
    )
    lane = lax.broadcasted_iota(jnp.int32, (queries, LANES), 1)
    tops = jnp.zeros((queries, LANES), F32)
    whole_row[...] = jnp.zeros(whole_row.shape, F32)
    for t in range(terms):
        part = found[t * queries : (t + 1) * queries]
        top = jnp.maximum(jnp.max(part, axis=1, keepdims=True), TINY)
        whole_row[:, :images] = part * (LEVELS / top) + 0.5
        coded[t] = (whole_row[...].astype(jnp.int32) - OFFSET).astype(jnp.int16)
        tops = jnp.where(lane == t, top * (1.0 / LEVELS), tops)
    scales[...] = jnp.swapaxes(tops, 0, 1)[: scales.shape[0]]
    for copy in leaving:
        copy.wait()


def score_slab(place, ids, weights, slab, terms, images, part, parts, coded):
    slots, queries = ids.shape[0], ids.shape[1] // parts
    groups = queries // GROUP
    share = pl.BlockSpec((slots, queries), lambda i, s: (0, part))
    held, width = slab.shape
    padded = -(-width // WIDE) * WIDE
    rows = queries * parts // terms
    given = [] if coded is None else [coded]
    span = (terms // parts, rows, images)
    kept = -(-(terms // parts) // 8) * 8
    return pl.pallas_call(
        score_kernel,
        grid_spec=pltpu.PrefetchScalarGridSpec(
            num_scalar_prefetch=1,
            grid=(1,),
            in_specs=[share, share, pl.BlockSpec(memory_space=pltpu.HBM)]
            + [pl.BlockSpec(memory_space=pl.ANY)] * len(given),
            out_specs=[
                pl.BlockSpec(memory_space=pl.ANY),
                pl.BlockSpec(span, lambda i, s: (part, 0, 0)),
                pl.BlockSpec((kept, rows), lambda i, s: (0, 0)),
            ],
            scratch_shapes=[
                pltpu.VMEM((queries, padded), BF16),
                pltpu.VMEM((rows, images), F32),
                pltpu.VMEM(slab.shape, BF16),
                pltpu.VMEM((queries, slots), jnp.int32),
                pltpu.VMEM((queries, slots), F32),
                pltpu.VMEM((groups, GROUP * slots), jnp.int32),
                pltpu.VMEM((groups, GROUP * slots), F32),
                pltpu.SemaphoreType.DMA,
                pltpu.SemaphoreType.DMA((4,)),
            ],
        ),
        out_shape=[
            pltpu.HBM((queries, padded), BF16),
            pltpu.HBM((terms, rows, images), jnp.int16),
            jax.ShapeDtypeStruct((kept, rows), F32),
        ],
        input_output_aliases={} if coded is None else {4: 1},
        compiler_params=pltpu.CompilerParams(vmem_limit_bytes=50 << 20),
        cost_estimate=pl.CostEstimate(flops=K1COST, bytes_accessed=1024, transcendentals=0),
        name="score_slab",
    )(place, ids, weights, pltpu.with_memory_space_constraint(slab, pltpu.HBM), *given)


def project_kernel(counts, block, images, patches, spans, offset, place, *refs):
    groups = []
    for count in counts:
        groups.append(refs[:count])
        refs = refs[count:]
    features, weights, dense = groups
    bias, running, out, rows, gathered, wide, came_f, came_w, came_d = refs
    depth, columns = weights[0].shape[0], gathered.shape[1]
    index = place[0]

    tiles = [(left, min(left + TILE, columns)) for left in range(0, columns, TILE)]
    if columns % LANES:
        tiles = [(0, columns)]

    def fetch_rows(j, k):
        left, right = tiles[j]
        at = pl.multiple_of(jnp.bitwise_xor(index, k) * depth, depth)
        return pltpu.make_async_copy(
            weights[k].at[:, spans[k] + left : spans[k] + right],
            gathered.at[pl.ds(at, depth), left:right],
            came_w.at[j, k],
        )

    def fetch_dense(j, k):
        left, right = tiles[j]
        if columns % LANES:
            return pltpu.make_async_copy(dense[k], wide.at[k], came_d.at[j, k])
        return pltpu.make_async_copy(
            dense[k].at[:, offset + left : offset + right],
            wide.at[k, :, left:right],
            came_d.at[j, k],
        )

    def start_features(first):
        for at, copy in features_in:
            if first <= at < first + block:
                copy.start()

    features_in, at = [], 0
    for k, source in enumerate(features):
        size = source.shape[0]
        copy = pltpu.make_async_copy(source, rows.at[at : at + size], came_f.at[k])
        features_in.append((at, copy))
        at += size
    for k in range(len(weights)):
        fetch_rows(0, k).start()
    start_features(0)
    queries, lines = out.shape[2], out.shape[1]
    sums = [None] * len(dense)

    def score(j, pooled):
        left, right = tiles[j]
        for k in range(len(dense)):
            part = lax.dot_general(
                pooled, wide[k, :, left:right], ROWS_BY_ROWS, preferred_element_type=F32
            )
            sums[k] = part if sums[k] is None else sums[k] + part

    pooled = None
    for j, (left, right) in enumerate(tiles):
        for k in range(len(weights)):
            fetch_rows(j, k).wait()
        if j:
            for k in range(len(dense)):
                fetch_dense(j - 1, k).wait()
        best = None
        for first in range(0, rows.shape[0], block):
            for at, copy in features_in:
                if not j and first <= at < first + block:
                    copy.wait()
            if not first:
                if not j:
                    for later in range(block, rows.shape[0], block):
                        start_features(later)
                    for k in range(len(dense)):
                        fetch_dense(0, k).start()
                if j + 1 < len(tiles):
                    for k in range(len(weights)):
                        fetch_rows(j + 1, k).start()
                    for k in range(len(dense)):
                        fetch_dense(j + 1, k).start()
            held = rows[first : first + block]
            real = held[:, 0:1].astype(F32) < jnp.inf
            logits = jnp.dot(held, gathered[:, left:right], preferred_element_type=F32)
            if j and not first:
                score(j - 1, pooled)
            logits = jnp.where(real, logits, -jnp.inf)
            logits = logits.reshape(-1, images, patches, right - left)
            tops = jnp.max(jnp.max(logits, axis=0), axis=1)
            best = tops if best is None else jnp.maximum(best, tops)
        active = jnp.log1p(jnp.maximum(best + bias[:, left:right], 0.0))
        pooled = jnp.concatenate([active, jnp.zeros_like(active)], axis=0).astype(BF16)
    for k in range(len(dense)):
        fetch_dense(len(tiles) - 1, k).wait()
    score(len(tiles) - 1, pooled)
    t = 0
    for found in sums:
        for left in range(0, found.shape[1], queries):
            out[t] = running[t] + found[:lines, left : left + queries]
            t += 1


def project(index, features, weights, spans, offset, bias, dense, running, images, patches):
    width = features[0].shape[1]
    columns = bias.shape[1]
    total = sum(f.shape[0] for f in features)
    block = 512 if total % 512 == 0 else total
    queries, padded = dense[0].shape
    tail = offset + columns >= padded - WIDE + 1 and columns % LANES
    kept = padded - offset if tail else columns
    inputs = [*features, *weights, *dense]
    local = pl.BlockSpec(memory_space=pltpu.VMEM)
    return pl.pallas_call(
        functools.partial(
            project_kernel,
            (len(features), len(weights), len(dense)),
            block,
            images,
            patches,
            spans,
            offset,
        ),
        in_specs=[pl.BlockSpec(memory_space=pltpu.SMEM)]
        + [pl.BlockSpec(memory_space=pl.ANY)] * len(inputs)
        + [local, local],
        out_specs=local,
        scratch_shapes=[
            pltpu.VMEM((total, width), BF16),
            pltpu.VMEM((width, columns), BF16),
            pltpu.VMEM((len(dense), queries, kept), BF16),
            pltpu.SemaphoreType.DMA((len(features),)),
            pltpu.SemaphoreType.DMA((-(-columns // TILE), len(weights))),
            pltpu.SemaphoreType.DMA((-(-columns // TILE), len(dense))),
        ],
        out_shape=jax.ShapeDtypeStruct(running.shape, F32),
        compiler_params=pltpu.CompilerParams(vmem_limit_bytes=40 << 20),
        cost_estimate=BRIEF,
        name="project",
    )(
        jnp.stack([index]).astype(jnp.int32),
        *[pltpu.with_memory_space_constraint(f, pltpu.HBM) for f in features],
        *weights,
        *dense,
        bias,
        running,
    )


def finish_kernel(images, coded, fresh, out, table, held, came):
    terms, queries, _ = coded.shape
    copies = [pltpu.make_async_copy(coded.at[t], held.at[t], came.at[t]) for t in range(terms)]
    for copy in copies:
        copy.start()
    total = None
    for t in range(fresh.shape[0]):
        part = fresh[t]
        total = part if total is None else total + part
    table[...] = jnp.zeros(table.shape, F32)
    table[LANES - images :, :queries] = total[:images]
    for t in range(terms):
        table[t : t + 1, :queries] = fresh[t][images : images + 1]
    columns = jnp.swapaxes(table[...], 0, 1)[:queries]
    stored = None
    for t in range(terms):
        copies[t].wait()
        part = (held[t].astype(jnp.int32) + OFFSET).astype(F32) * columns[:, t : t + 1]
        stored = part if stored is None else stored + part
    out[...] = stored
    tail = out.shape[1] - LANES
    lane = lax.broadcasted_iota(jnp.int32, (queries, LANES), 1)
    out[:, tail:] = jnp.where(lane < LANES - images, stored[:, tail:], columns)


def finish(coded, fresh, images):
    terms, queries, total = coded.shape
    local = pl.BlockSpec(memory_space=pltpu.VMEM)
    return pl.pallas_call(
        functools.partial(finish_kernel, images),
        in_specs=[pl.BlockSpec(memory_space=pl.ANY), local],
        out_specs=local,
        scratch_shapes=[
            pltpu.VMEM((LANES, LANES), F32),
            pltpu.VMEM(coded.shape, jnp.int16),
            pltpu.SemaphoreType.DMA((terms,)),
        ],
        out_shape=jax.ShapeDtypeStruct((queries, total), F32),
        compiler_params=pltpu.CompilerParams(vmem_limit_bytes=16 << 20),
        cost_estimate=BRIEF,
        name="finish",
    )(coded, fresh)


def column_blocks(width):
    if width % LANES or width < 8 * LANES:
        return [(0, width)]
    tiles = width // LANES
    small = max(1, tiles * 2 // 15)
    sizes = [tiles * 8 // 30, tiles - tiles * 8 // 30 - small, small]
    return [(sum(sizes[:i]) * LANES, size * LANES) for i, size in enumerate(sizes)]


def shards(rows, terms, patches, patch_mask, proj_weight, proj_bias, slab, query_ids, term_weights):
    along_x = 1
    while along_x * along_x * 4 <= terms:
        along_x *= 2
    along_z = terms // along_x
    row, core, term = lax.axis_index("row"), lax.axis_index("core"), lax.axis_index("term")
    images, patch_rows, features = patches.shape
    width = proj_weight.shape[1]
    held = slab.shape[0]
    block_queries = query_ids.shape[0] // terms

    def to_term(value, k):
        return lax.ppermute(value, "term", [(i, i ^ k) for i in range(terms)])

    def to_row(value, k):
        return lax.ppermute(value, "row", [(i, i ^ k) for i in range(rows)])

    def to_core(value):
        return lax.ppermute(value, "core", [(0, 1), (1, 0)])

    def after(value, *done):
        return lax.optimization_barrier((value, done))[0]

    blocks = column_blocks(width)
    crossed, local = [], []
    for b, (start, size) in enumerate(blocks):
        sent = proj_weight[:, start : start + size]
        local.append(sent)
        crossed.append([to_row(sent, k) for k in range(1, rows)])
        if not b:
            patches = after(patches, sent)

    marked = jnp.where(patch_mask[:, :, None] > 0, patches, jnp.array(jnp.inf, BF16))
    marked = marked.reshape(images * patch_rows, features)
    first_x = [to_term(marked, k) for k in range(1, along_x)]
    by_z = []
    for k in range(1, along_z):
        near = k & -k
        by_z.append(to_term(by_z[k - near - 1] if k > near else marked, near * along_x))
    second_x = [[to_term(block, k) for block in by_z] for k in range(1, along_x)]
    gathered = [marked, *by_z, *first_x]
    for blocks_x in second_x:
        gathered += blocks_x

    place = jnp.stack([term * width]).astype(jnp.int32)
    dense, scales, coded = [], [], None
    for part in range(PARTS):
        here = after(place, by_z[:1], first_x, [v[:1] for v in second_x], local[-1]) if part else place
        full, coded, scale = score_slab(
            here, query_ids.T, term_weights.T, slab, terms, held + images, part, PARTS, coded
        )
        dense.append(pltpu.with_memory_space_constraint(full, pltpu.HBM))
        scales.append(scale[: terms // PARTS])
    swapped = [to_core(part) for part in after(crossed[0], by_z)]
    coded = after(coded, swapped, second_x)
    coded = lax.all_to_all(coded, "term", split_axis=0, concat_axis=0, tiled=True)

    scales = jnp.concatenate(scales).reshape(terms, 1, block_queries)
    running = jnp.concatenate(
        [jnp.zeros((terms, images, block_queries), F32), scales,
         jnp.zeros((terms, 7 - images, block_queries), F32)], axis=1)
    bias = proj_bias.reshape(1, width)
    beside = to_core(after(proj_weight, by_z))
    for b, (start, size) in enumerate(blocks):
        if 0 < b < len(blocks) - 1:
            swapped = [to_core(part) for part in crossed[b]]
        pieces = [local[b], beside]
        for mine, other in zip(crossed[b], swapped):
            pieces += [mine, other]
        spans = [0, start] + [0] * (len(pieces) - 2)
        running = project(
            2 * row + core, gathered, pieces, spans, start, bias[:, start : start + size],
            dense, running, images, patch_rows,
        )
        if b == len(blocks) - 3:
            swapped_last = [to_core(part) for part in after(crossed[-1], running)]
            running = after(running, crossed[-1])
        if b == len(blocks) - 2:
            swapped = swapped_last
    running, coded = lax.optimization_barrier((running, coded))
    fresh = lax.all_to_all(running, "term", split_axis=0, concat_axis=0, tiled=True)
    return finish(coded, fresh, images)


def solution(mesh):
    groups, terms = mesh.shape["img"], mesh.shape["term"]
    rows = groups // 2
    cores = Mesh(mesh.devices.reshape(rows, 2, terms), ("row", "core", "term"))
    img = ("row", "core")
    placed = (
        P(img, "term", None),
        P(img, "term"),
        P(img, "term"),
        P("term"),
        P(img, "term"),
        P(),
        P(),
    )
    return jax.shard_map(
        functools.partial(shards, rows, terms),
        mesh=cores,
        in_specs=placed,
        out_specs=P("term", img),
        check_vma=False,
    )
```
